256 devices in a mesh: row: 16 (over z, core), col: 16 (over y, x).
Axes of the slice: x: 4, y: 4, z: 8, core: 2. Of those that a mesh axis runs over, the one named last changes fastest.
Arguments:
- tokens: bfloat16 [1024, 12288], P('col', 'row'), may hold values from -6 to 6
- weight: bfloat16 [12288, 24576], P('row', 'col'), may hold values from -0.0546875 to 0.0546875
- cotangent: bfloat16 [1024, 24576], P('row', 'col'), may hold values from -6 to 6
Outputs:
- activated: bfloat16 [1024, 24576], P('row', 'col')
- input_grad: bfloat16 [1024, 12288], P('col', 'row')
- weight_grad: bfloat16 [12288, 24576], P('row', 'col')
The draws below stay inside these ranges and needn't reach their ends.
All inputs are finite; a program needn't handle non-finite values.
Results may differ from the reference program's by a relative error of at most 0.03.
Values may be sent and summed in bfloat16 or wider, within the bound.
A program may use at most 64 MiB of HBM per device.

```python
import math
import jax
import jax.numpy as jnp
from jax import lax

D = 12288
FF = 24576
TOKENS = 1024
N_ROW = 16
N_COL = 16


def levels(stream_key, extent, split, low, high):
    gain = 1.0
    for axis_at, parts in split:
        heights = jax.random.uniform(jax.random.fold_in(jax.random.fold_in(stream_key, 6), axis_at), (parts,), jnp.float32, low / len(split), high / len(split))
        gain = gain * jnp.repeat(jnp.exp(heights), extent[axis_at] // parts).reshape((-1,) + (1,) * (len(extent) - 1 - axis_at))
    return gain


def scatter_about(stream_key, shape, spread, bound, pieces=(), held_as=jnp.bfloat16):
    gain = levels(stream_key, shape, pieces, -0.22, 0.18) if pieces else 1.0
    array = jax.random.normal(stream_key, shape, jnp.float32) * spread * gain
    return jnp.minimum(jnp.maximum(array, -bound), bound).astype(held_as)


def setup_inputs(seed: int = 0) -> dict:
    splits = jax.random.split(jax.random.key(seed), 4)
    tokens = scatter_about(splits[0], (TOKENS, D), 1.0, 6.0, ((0, 16), (1, 16)))
    weight = scatter_about(splits[1], (D, FF), D ** -0.5, 0.0546875, ((0, 16), (1, 16)))
    cotangent = scatter_about(splits[2], (TOKENS, FF), 1.0, 6.0, ((0, 16), (1, 16)))
    return {"tokens": tokens, "weight": weight, "cotangent": cotangent}


def gelu_exact(value):
    return 0.5 * value * (1.0 + jax.scipy.special.erf(value / math.sqrt(2.0)))

def gelu_slope(value):
    return 0.5 * (1.0 + jax.scipy.special.erf(value / math.sqrt(2.0))) + value * jnp.exp(-0.5 * value * value) / math.sqrt(2.0 * math.pi)

def reference(tokens, weight, cotangent):
    width_block = D // N_ROW
    unit_block = FF // N_COL

    def forward_step(total, index):
        start = (index * width_block).astype(jnp.int32)
        left = lax.dynamic_slice_in_dim(tokens, start, width_block, 1)
        right = lax.dynamic_slice_in_dim(weight, start, width_block, 0)
        partial_sum = jnp.dot(left, right, preferred_element_type=jnp.float32)
        rounded = lax.optimization_barrier(partial_sum.astype(jnp.bfloat16))
        return (total + rounded.astype(jnp.float32), None)
    pre, _ = lax.scan(forward_step, jnp.zeros((TOKENS, FF), jnp.float32), jnp.arange(N_ROW, dtype=jnp.int32))
    activated = gelu_exact(pre).astype(jnp.bfloat16)
    slope_grad = (cotangent.astype(jnp.float32) * gelu_slope(pre)).astype(jnp.bfloat16)

    def back_step(total, index):
        start = (index * unit_block).astype(jnp.int32)
        left = lax.dynamic_slice_in_dim(slope_grad, start, unit_block, 1)
        right = lax.dynamic_slice_in_dim(weight, start, unit_block, 1)
        partial_sum = lax.dot_general(left, right, (((1,), (1,)), ((), ())), preferred_element_type=jnp.float32)
        rounded = lax.optimization_barrier(partial_sum.astype(jnp.bfloat16))
        return (total + rounded.astype(jnp.float32), None)
    back_total, _ = lax.scan(back_step, jnp.zeros((TOKENS, D), jnp.float32), jnp.arange(N_COL, dtype=jnp.int32))
    input_grad = back_total.astype(jnp.bfloat16)
    weight_grad = lax.dot_general(tokens, slope_grad, (((0,), (0,)), ((), ())), preferred_element_type=jnp.float32).astype(jnp.bfloat16)
    return (activated, input_grad, weight_grad)
```

```python
import functools
import math

import jax
import jax.numpy as jnp
from jax import lax
from jax.experimental import pallas as pl
from jax.experimental.pallas import tpu as pltpu
from jax.sharding import PartitionSpec as P

MESH = pl.DeviceIdType.MESH
BF16 = jnp.bfloat16
F32 = jnp.float32

NR = 16
NC = 16
NZ = NR // 2
ROWS = 16
TILE = 256


def gelu_pair(value):
    phi = 0.5 * (1.0 + lax.erf(value * (1.0 / math.sqrt(2.0))))
    slope = phi + value * jnp.exp(-0.5 * value * value) * (1.0 / math.sqrt(2.0 * math.pi))
    return value * phi, slope


def kernel(
    stages,
    tok_ref, w_ref, cot_ref,
    act_ref, ig_ref, wg_ref,
    w, cot, tok, pp, px, s4, sp, sm, rp, rm, g, ip, r2, act, ig, wg,
    in_sem, out_sem,
    ag1_send, ag1_recv, px_send, px_recv,
    rs_send, rp_recv, rm_recv,
    ag_send, gp_recv, gm_recv, pt_send, pt_recv,
    r2_send, r2_recv,
):
    r, c = lax.axis_index("row"), lax.axis_index("col")
    z, k = r // 2, lax.rem(r, 2)
    other = 1 - k
    width, hidden = w.shape
    half = hidden // 2
    lo, hi = pl.ds(0, half), pl.ds(half, half)

    up = (lax.rem(r + 2, NR), c)
    down = (lax.rem(r + NR - 2, NR), c)
    partner = (r + 1 - 2 * k, c)

    def peer(i):
        return lax.rem(c + i, NC)

    def at_z(q):
        return lax.rem(z + q + NZ, NZ)

    def remote(src, dst, ss, rs, dev):
        cp = pltpu.make_async_remote_copy(
            src_ref=src, dst_ref=dst, send_sem=ss, recv_sem=rs,
            device_id=dev, device_id_type=MESH,
        )
        cp.start()

    def wait_for(ref, sem):
        pltpu.make_async_copy(ref, ref, sem).wait()

    loads = [
        pltpu.make_async_copy(w_ref, w, in_sem.at[0]),
        pltpu.make_async_copy(cot_ref, cot, in_sem.at[1]),
    ]
    for cp in loads:
        cp.start()

    barrier = pltpu.get_barrier_semaphore()
    greeted = [(r, peer(i)) for i in range(1, NC)] + [up, down, partner]
    for dev in greeted:
        pl.semaphore_signal(barrier, inc=1, device_id=dev, device_id_type=MESH)
    pl.semaphore_wait(barrier, len(greeted))

    for s in range(stages):
        block = tok_ref.at[pl.ds(s * ROWS, ROWS)]
        for i in range(1, NC):
            remote(block, tok.at[s, c], ag1_send.at[s], ag1_recv.at[s], (r, peer(i)))
        own = pltpu.make_async_copy(block, tok.at[s, c], in_sem.at[2 + s])
        own.start()
        loads.append(own)

    def m1(s):
        if s == 0:
            loads[0].wait()
        loads[2 + s].wait()
        wait_for(tok.at[s, pl.ds(0, NC - 1)], ag1_recv.at[s])

        def body(j, carry):
            cols = pl.ds(pl.multiple_of(j * TILE, TILE), TILE)
            left = tok[s].reshape(NC * ROWS, width)
            part = jnp.dot(left, w[:, cols], preferred_element_type=F32).astype(BF16)
            pp[s, :, :, :, cols] = part.reshape(NZ, 2, ROWS, TILE)
            return carry

        lax.fori_loop(0, hidden // TILE, body, 0)
        remote(pp.at[s, :, other], px.at[s], px_send.at[s], px_recv.at[s], partner)

    def base(s, d):
        return pp[s, d, k].astype(F32) + px[s, d].astype(F32)

    def r4(s):
        wait_for(px.at[s], px_recv.at[s])
        s4[s] = base(s, at_z(4)).astype(BF16)
        remote(s4.at[s, :, lo], rp.at[s, 3, :, lo], rs_send.at[s, 0], rp_recv.at[s, 3], up)
        remote(s4.at[s, :, hi], rm.at[s, 3, :, hi], rs_send.at[s, 1], rm_recv.at[s, 3], down)

    def r3(s):
        wait_for(rp.at[s, 3, :, lo], rp_recv.at[s, 3])
        up_sum = base(s, at_z(3))
        sp[s, 3, :, lo] = (up_sum[:, :half] + rp[s, 3, :, lo].astype(F32)).astype(BF16)
        sp[s, 3, :, hi] = up_sum[:, half:].astype(BF16)
        remote(sp.at[s, 3], rp.at[s, 2], rs_send.at[s, 2], rp_recv.at[s, 2], up)
        wait_for(rm.at[s, 3, :, hi], rm_recv.at[s, 3])
        down_sum = base(s, at_z(-3))
        sm[s, 3, :, hi] = (down_sum[:, half:] + rm[s, 3, :, hi].astype(F32)).astype(BF16)
        sm[s, 3, :, lo] = down_sum[:, :half].astype(BF16)
        remote(sm.at[s, 3], rm.at[s, 2], rs_send.at[s, 3], rm_recv.at[s, 2], down)

    def rj(s, j):
        wait_for(rp.at[s, j], rp_recv.at[s, j])
        sp[s, j] = (base(s, at_z(j)) + rp[s, j].astype(F32)).astype(BF16)
        remote(sp.at[s, j], rp.at[s, j - 1], rs_send.at[s, 8 - 2 * j], rp_recv.at[s, j - 1], up)
        wait_for(rm.at[s, j], rm_recv.at[s, j])
        sm[s, j] = (base(s, at_z(-j)) + rm[s, j].astype(F32)).astype(BF16)
        remote(sm.at[s, j], rm.at[s, j - 1], rs_send.at[s, 9 - 2 * j], rm_recv.at[s, j - 1], down)

    def r0(s):
        wait_for(rp.at[s, 0], rp_recv.at[s, 0])
        wait_for(rm.at[s, 0], rm_recv.at[s, 0])
        if s == 0:
            loads[1].wait()
        rows = pl.ds(s * ROWS, ROWS)
        pre = base(s, z) + rp[s, 0].astype(F32) + rm[s, 0].astype(F32)
        activated, slope = gelu_pair(pre)
        g[s, z, k] = (cot[rows].astype(F32) * slope).astype(BF16)
        mine = g.at[s, z, k]
        remote(mine, mine, ag_send.at[s, 0], gp_recv.at[s, 0], up)
        remote(mine, mine, ag_send.at[s, 1], gm_recv.at[s, 0], down)
        remote(mine, mine, pt_send.at[s], pt_recv.at[s], partner)
        act[rows] = activated.astype(BF16)

    def a(s, j):
        below, above = g.at[s, at_z(-j), k], g.at[s, at_z(j), k]
        if j < 3:
            wait_for(below, gp_recv.at[s, j - 1])
            remote(below, below, ag_send.at[s, 2 * j], gp_recv.at[s, j], up)
            wait_for(above, gm_recv.at[s, j - 1])
            remote(above, above, ag_send.at[s, 2 * j + 1], gm_recv.at[s, j], down)
        else:
            wait_for(below, gp_recv.at[s, j - 1])
            part = g.at[s, at_z(-j), k, :, lo]
            remote(part, part, ag_send.at[s, 2 * j], gp_recv.at[s, j], up)
            wait_for(above, gm_recv.at[s, j - 1])
            part = g.at[s, at_z(j), k, :, hi]
            remote(part, part, ag_send.at[s, 2 * j + 1], gm_recv.at[s, j], down)
        remote(below, below, pt_send.at[s], pt_recv.at[s], partner)
        remote(above, above, pt_send.at[s], pt_recv.at[s], partner)

    def a4(s):
        far = g.at[s, at_z(4), k]
        wait_for(g.at[s, at_z(4), k, :, lo], gp_recv.at[s, 3])
        wait_for(g.at[s, at_z(4), k, :, hi], gm_recv.at[s, 3])
        remote(far, far, pt_send.at[s], pt_recv.at[s], partner)

    def m2(s):
        wait_for(g.at[s, :, other], pt_recv.at[s])

        def body(j, carry):
            cols = pl.ds(pl.multiple_of(j * TILE, TILE), TILE)
            left = g[s].reshape(NR * ROWS, hidden)
            part = lax.dot_general(
                left, w[cols, :], (((1,), (1,)), ((), ())), preferred_element_type=F32
            ).astype(BF16)
            ip[s, :, :, cols] = part.reshape(NC, ROWS, TILE)
            return carry

        lax.fori_loop(0, width // TILE, body, 0)
        for i in range(1, NC):
            remote(ip.at[s, peer(i)], r2.at[s, i - 1], r2_send.at[s], r2_recv.at[s], (r, peer(i)))

    def fin(s):
        wait_for(r2.at[s], r2_recv.at[s])
        total = ip[s, c].astype(F32)
        for i in range(NC - 1):
            total += r2[s, i].astype(F32)
        ig[pl.ds(s * ROWS, ROWS)] = total.astype(BF16)

    def wgrad():
        def body(j, carry):
            cols = pl.ds(pl.multiple_of(j * TILE, TILE), TILE)
            left = tok[...].reshape(stages * NC * ROWS, width)
            right = g[:, :, :, :, cols].reshape(stages * NR * ROWS, TILE)
            wg[:, cols] = lax.dot_general(
                left, right, (((0,), (0,)), ((), ())), preferred_element_type=F32
            ).astype(BF16)
            return carry

        lax.fori_loop(0, hidden // TILE, body, 0)

    steps = [
        m1, r4, r3,
        lambda s: rj(s, 2), lambda s: rj(s, 1), r0,
        lambda s: a(s, 1), lambda s: a(s, 2), lambda s: a(s, 3), a4, m2,
    ]
    for t in range(len(steps) + stages - 1):
        for s in range(stages):
            if 0 <= t - s < len(steps):
                steps[t - s](s)
    outs = [pltpu.make_async_copy(act, act_ref, out_sem.at[0])]
    outs[0].start()
    wgrad()
    outs.append(pltpu.make_async_copy(wg, wg_ref, out_sem.at[1]))
    outs[1].start()
    for s in range(stages):
        fin(s)
    outs.append(pltpu.make_async_copy(ig, ig_ref, out_sem.at[2]))
    outs[2].start()

    for s in range(stages):
        wait_for(tok.at[s, pl.ds(0, NC - 1)], ag1_send.at[s])
        wait_for(px.at[s], px_send.at[s])
        wait_for(s4.at[s, :, lo], rs_send.at[s, 0])
        wait_for(s4.at[s, :, hi], rs_send.at[s, 1])
        for j in range(2, 8):
            wait_for(s4.at[s], rs_send.at[s, j])
        for j in range(6):
            wait_for(s4.at[s], ag_send.at[s, j])
        wait_for(s4.at[s, :, lo], ag_send.at[s, 6])
        wait_for(s4.at[s, :, hi], ag_send.at[s, 7])
        wait_for(g.at[s, :, 0], pt_send.at[s])
        wait_for(r2.at[s], r2_send.at[s])
    for cp in outs:
        cp.wait()


def on_device(tokens, weight, cotangent):
    rows, width = tokens.shape
    hidden = weight.shape[1]
    stages = rows // ROWS
    vmem, dma = pltpu.VMEM, pltpu.SemaphoreType.DMA
    any_spec = pl.BlockSpec(memory_space=pl.ANY)
    return tuple(pl.pallas_call(
        functools.partial(kernel, stages),
        out_shape=(
            jax.ShapeDtypeStruct((rows, hidden), BF16),
            jax.ShapeDtypeStruct((rows, width), BF16),
            jax.ShapeDtypeStruct((width, hidden), BF16),
        ),
        in_specs=[any_spec] * 3,
        out_specs=(any_spec,) * 3,
        scratch_shapes=[
            vmem((width, hidden), BF16),
            vmem((rows, hidden), BF16),
            vmem((stages, NC, ROWS, width), BF16),
            vmem((stages, NZ, 2, ROWS, hidden), BF16),
            vmem((stages, NZ, ROWS, hidden), BF16),
            vmem((stages, ROWS, hidden), BF16),
            vmem((stages, 4, ROWS, hidden), BF16),
            vmem((stages, 4, ROWS, hidden), BF16),
            vmem((stages, 4, ROWS, hidden), BF16),
            vmem((stages, 4, ROWS, hidden), BF16),
            vmem((stages, NZ, 2, ROWS, hidden), BF16),
            vmem((stages, NC, ROWS, width), BF16),
            vmem((stages, NC - 1, ROWS, width), BF16),
            vmem((rows, hidden), BF16),
            vmem((rows, width), BF16),
            vmem((width, hidden), BF16),
            dma((2 + stages,)), dma((3,)),
            dma((stages,)), dma((stages,)), dma((stages,)), dma((stages,)),
            dma((stages, 8)), dma((stages, 4)), dma((stages, 4)),
            dma((stages, 8)), dma((stages, 4)), dma((stages, 4)),
            dma((stages,)), dma((stages,)),
            dma((stages,)), dma((stages,)),
        ],
        compiler_params=pltpu.CompilerParams(
            collective_id=0, has_side_effects=True, vmem_limit_bytes=56 * 2**20
        ),
        name="updown",
    )(tokens, weight, cotangent))


def solution(mesh):
    return jax.shard_map(
        on_device,
        mesh=mesh,
        in_specs=(P("col", "row"), P("row", "col"), P("row", "col")),
        out_specs=(P("row", "col"), P("col", "row"), P("row", "col")),
        check_vma=False,
    )
```

```python
import functools
import math

import jax
import jax.numpy as jnp
from jax import lax
from jax.experimental import pallas as pl
from jax.experimental.pallas import tpu as pltpu
from jax.sharding import PartitionSpec as P

MESH = pl.DeviceIdType.MESH
BF16 = jnp.bfloat16
F32 = jnp.float32

NR = 16
NC = 16
NZ = NR // 2
ROWS = 16
TILE = 512

CUTS = {1: ((0, 1, 2, 3, 4),), 2: ((0, 1, 2), (3, 4)), 3: ((0, 1, 2), (3,), (4,)), 4: ((0, 1), (2,), (3,), (4,))}
PIECES = (1, 1, 1, 1)
TWO = (1, 1, 1, 1)
DIRECT = (0, 0, 0, 0)
ORDER = (
    ("O", 0), ("O", 1), ("O", 2), ("O", 3), ("F", 0), ("F", 1), ("F", 2), ("F", 3), ("M", 0), ("M", 1),
    ("R4", 0), ("M", 2), ("R4", 1), ("M", 3), ("R3", 0), ("R4", 2), ("R3", 1), ("R4", 3), ("R2", 0), ("R3", 2),
    ("R2", 1), ("R3", 3), ("R1", 0), ("R2", 2), ("R1", 1), ("R2", 3), ("R0", 0), ("R1", 2), ("R0", 1),
    ("R1", 3), ("A1", 0), ("R0", 2), ("A1", 1), ("R0", 3), ("A2", 0), ("A1", 2), ("A2", 1), ("A1", 3),
    ("A3", 0), ("A2", 2), ("A3", 1), ("A2", 3), ("A4", 0), ("A3", 2), ("A4", 1), ("A3", 3), ("N0", 0),
    ("A4", 2), ("N0", 1), ("A4", 3), ("N0", 2), ("WG", 0), ("P", 0), ("N0", 3), ("P", 1), ("P", 2), ("P", 3),
    ("WG", 1), ("FIN", 0), ("FIN", 1), ("FIN", 2), ("FIN", 3),
)


def gelu_pair(value):
    phi = 0.5 * (1.0 + lax.erf(value * (1.0 / math.sqrt(2.0))))
    slope = phi + value * jnp.exp(-0.5 * value * value) * (1.0 / math.sqrt(2.0 * math.pi))
    return value * phi, slope


def kernel(
    stages,
    tok_ref, w_ref, cot_ref,
    act_ref, ig_ref, wg_ref,
    w, cot, tok, pp, px, s4, sp, sm, rp, rm, g, ip, r2, t0, t1, act, ig, wg, acc,
    in_sem, out_sem,
    ag1_send, ag1a_recv, ag1b_recv, px_send, px_recv,
    rs_send, rp_recv, rm_recv,
    ag_send, gp_recv, gm_recv, pt_send, pt_recv,
    r2_send, r2_recv, r2b_send, r2b_recv,
):
    r, c = lax.axis_index("row"), lax.axis_index("col")
    z, k = r // 2, lax.rem(r, 2)
    other = 1 - k
    width, hidden = w.shape
    half = hidden // 2
    lo, hi = pl.ds(0, half), pl.ds(half, half)

    up = (lax.rem(r + 2, NR), c)
    down = (lax.rem(r + NR - 2, NR), c)
    partner = (r + 1 - 2 * k, c)

    def peer(i):
        return lax.rem(c + i, NC)

    def shift(da, db):
        dx, dy = da + k * (db - da), db + k * (da - db)
        return lax.rem(c // 4 + dy + 4, 4) * 4 + lax.rem(c + dx + 4, 4)

    def at_z(q):
        return lax.rem(z + q + NZ, NZ)

    def remote(src, dst, ss, rs, dev):
        cp = pltpu.make_async_remote_copy(
            src_ref=src, dst_ref=dst, send_sem=ss, recv_sem=rs,
            device_id=dev, device_id_type=MESH,
        )
        cp.start()

    def wait_for(ref, sem):
        pltpu.make_async_copy(ref, ref, sem).wait()

    loads = [
        pltpu.make_async_copy(w_ref, w, in_sem.at[0]),
        pltpu.make_async_copy(cot_ref, cot, in_sem.at[1]),
    ]
    for cp in loads:
        cp.start()

    barrier = pltpu.get_barrier_semaphore()
    if any(DIRECT) or not all(TWO):
        greeted = [(r, peer(i)) for i in range(1, NC)]
    else:
        greeted = [(r, shift(i, 0)) for i in (1, 2, 3)] + [(r, shift(0, i)) for i in (1, 2, 3)]
    greeted += [up, down, partner]
    for dev in greeted:
        pl.semaphore_signal(barrier, inc=1, device_id=dev, device_id_type=MESH)
    pl.semaphore_wait(barrier, len(greeted))

    own_copies = {}

    def own(s):
        block = tok_ref.at[pl.ds(s * ROWS, ROWS)]
        if DIRECT[s]:
            for i in range(1, NC):
                remote(block, tok.at[s, c], ag1_send.at[s], ag1b_recv.at[s], (r, peer(i)))
        else:
            for i in (1, 3, 2):
                remote(block, tok.at[s, c], ag1_send.at[s], ag1a_recv.at[s, i - 1], (r, shift(i, 0)))
            for i in (1, 3, 2):
                remote(block, tok.at[s, c], ag1_send.at[s], ag1b_recv.at[s], (r, shift(0, i)))
        cp = pltpu.make_async_copy(block, tok.at[s, c], in_sem.at[2 + s])
        cp.start()
        own_copies[s] = cp

    def forward(s):
        for i in (1, 3, 2):
            block = tok.at[s, shift(-i, 0)]
            wait_for(block, ag1a_recv.at[s, i - 1])
            for j in (1, 3, 2):
                remote(block, block, ag1_send.at[s], ag1b_recv.at[s], (r, shift(0, j)))

    def m1(s):
        if s == 0:
            loads[0].wait()
        own_copies[s].wait()
        wait_for(tok.at[s, pl.ds(0, 15 if DIRECT[s] else 12)], ag1b_recv.at[s])
        left = tok[s].reshape(NC * ROWS, width)
        part = jnp.dot(left, w[...], preferred_element_type=F32).astype(BF16)
        pp[s] = part.reshape(NZ, 2, ROWS, hidden)
        remote(pp.at[s, :, other], px.at[s], px_send.at[s], px_recv.at[s], partner)

    def base(s, d):
        return pp[s, d, k].astype(F32) + px[s, d].astype(F32)

    def r4(s):
        wait_for(px.at[s], px_recv.at[s])
        s4[s] = base(s, at_z(4)).astype(BF16)
        remote(s4.at[s, :, lo], rp.at[s, 3, :, lo], rs_send.at[s, 0], rp_recv.at[s, 3], up)
        remote(s4.at[s, :, hi], rm.at[s, 3, :, hi], rs_send.at[s, 1], rm_recv.at[s, 3], down)

    def r3(s):
        wait_for(rp.at[s, 3, :, lo], rp_recv.at[s, 3])
        up_sum = base(s, at_z(3))
        sp[s, 3, :, lo] = (up_sum[:, :half] + rp[s, 3, :, lo].astype(F32)).astype(BF16)
        sp[s, 3, :, hi] = up_sum[:, half:].astype(BF16)
        remote(sp.at[s, 3], rp.at[s, 2], rs_send.at[s, 2], rp_recv.at[s, 2], up)
        wait_for(rm.at[s, 3, :, hi], rm_recv.at[s, 3])
        down_sum = base(s, at_z(-3))
        sm[s, 3, :, hi] = (down_sum[:, half:] + rm[s, 3, :, hi].astype(F32)).astype(BF16)
        sm[s, 3, :, lo] = down_sum[:, :half].astype(BF16)
        remote(sm.at[s, 3], rm.at[s, 2], rs_send.at[s, 3], rm_recv.at[s, 2], down)

    def rj(s, j):
        wait_for(rp.at[s, j], rp_recv.at[s, j])
        sp[s, j] = (base(s, at_z(j)) + rp[s, j].astype(F32)).astype(BF16)
        remote(sp.at[s, j], rp.at[s, j - 1], rs_send.at[s, 8 - 2 * j], rp_recv.at[s, j - 1], up)
        wait_for(rm.at[s, j], rm_recv.at[s, j])
        sm[s, j] = (base(s, at_z(-j)) + rm[s, j].astype(F32)).astype(BF16)
        remote(sm.at[s, j], rm.at[s, j - 1], rs_send.at[s, 9 - 2 * j], rm_recv.at[s, j - 1], down)

    def r0(s):
        wait_for(rp.at[s, 0], rp_recv.at[s, 0])
        wait_for(rm.at[s, 0], rm_recv.at[s, 0])
        if s == 0:
            loads[1].wait()
        rows = pl.ds(s * ROWS, ROWS)
        pre = base(s, z) + rp[s, 0].astype(F32) + rm[s, 0].astype(F32)
        activated, slope = gelu_pair(pre)
        g[s, z, k] = (cot[rows].astype(F32) * slope).astype(BF16)
        mine = g.at[s, z, k]
        remote(mine, mine, ag_send.at[s, 0], gp_recv.at[s, 0], up)
        remote(mine, mine, ag_send.at[s, 1], gm_recv.at[s, 0], down)
        remote(mine, mine, pt_send.at[s], pt_recv.at[s, 0], partner)
        act[rows] = activated.astype(BF16)

    def a(s, j):
        below, above = g.at[s, at_z(-j), k], g.at[s, at_z(j), k]
        if j < 3:
            wait_for(below, gp_recv.at[s, j - 1])
            remote(below, below, ag_send.at[s, 2 * j], gp_recv.at[s, j], up)
            wait_for(above, gm_recv.at[s, j - 1])
            remote(above, above, ag_send.at[s, 2 * j + 1], gm_recv.at[s, j], down)
        else:
            wait_for(below, gp_recv.at[s, j - 1])
            part = g.at[s, at_z(-j), k, :, lo]
            remote(part, part, ag_send.at[s, 2 * j], gp_recv.at[s, j], up)
            wait_for(above, gm_recv.at[s, j - 1])
            part = g.at[s, at_z(j), k, :, hi]
            remote(part, part, ag_send.at[s, 2 * j + 1], gm_recv.at[s, j], down)
        remote(below, below, pt_send.at[s], pt_recv.at[s, 2 * j - 1], partner)
        remote(above, above, pt_send.at[s], pt_recv.at[s, 2 * j], partner)

    def a4(s):
        far = g.at[s, at_z(4), k]
        wait_for(g.at[s, at_z(4), k, :, lo], gp_recv.at[s, 3])
        wait_for(g.at[s, at_z(4), k, :, hi], gm_recv.at[s, 3])
        remote(far, far, pt_send.at[s], pt_recv.at[s, 7], partner)

    def spread(s):
        left = g[s].reshape(NR * ROWS, hidden)
        part = lax.dot_general(
            left, w[...], (((1,), (1,)), ((), ())), preferred_element_type=F32
        ).astype(BF16)
        ip[s] = part.reshape(NC, ROWS, width)
        for i in (1, 3, 2):
            for j in range(4):
                remote(
                    ip.at[s, shift(i, j)], r2.at[s, 4 * i - 4 + j],
                    r2_send.at[s], r2_recv.at[s], (r, shift(i, 0)),
                )

    def pass_on(s):
        wait_for(r2.at[s, pl.ds(0, 12)], r2_recv.at[s])
        for j in (1, 3, 2, 0):
            total = ip[s, shift(0, j)].astype(F32)
            for i in range(3):
                total += r2[s, 4 * i + j].astype(F32)
            if j == 0:
                t0[s] = total
            else:
                t1[s, j - 1] = total.astype(BF16)
                remote(t1.at[s, j - 1], r2.at[s, 11 + j], r2b_send.at[s], r2b_recv.at[s], (r, shift(0, j)))

    def m2_part(s, chunks):
        for q, slot in chunks:
            wait_for(g.at[s, 0, 0], pt_recv.at[s, slot])
        if TWO[s]:
            return spread(s)
        left = jnp.concatenate(
            [g[s, at_z(q)].reshape(2 * ROWS, hidden) for q, _ in chunks], axis=0
        )
        part = lax.dot_general(
            left, w[...], (((1,), (1,)), ((), ())), preferred_element_type=F32
        ).astype(BF16)
        part = part.reshape(len(chunks), 2, ROWS, width)
        for n, (q, _) in enumerate(chunks):
            d = at_z(q)
            ip[s, pl.ds(2 * d, 2)] = part[n]
            for m in range(2):
                dest = 2 * d + m

                @pl.when(dest != c)
                def _():
                    slot = lax.rem(dest - c + NC, NC) - 1
                    remote(ip.at[s, dest], r2.at[s, slot], r2_send.at[s], r2_recv.at[s], (r, dest))

    def fin(s):
        if TWO[s]:
            wait_for(r2.at[s, pl.ds(12, 3)], r2b_recv.at[s])
            total = t0[s]
            for j in range(3):
                total += r2[s, 12 + j].astype(F32)
            ig[pl.ds(s * ROWS, ROWS)] = total.astype(BF16)
            return
        wait_for(r2.at[s], r2_recv.at[s])
        total = ip[s, c].astype(F32)
        for i in range(NC - 1):
            total += r2[s, i].astype(F32)
        ig[pl.ds(s * ROWS, ROWS)] = total.astype(BF16)

    def wgrad(part):
        some = pl.ds(2 * part, 2)

        def body(j, carry):
            cols = pl.ds(pl.multiple_of(j * TILE, TILE), TILE)
            left = tok[some].reshape(2 * NC * ROWS, width)
            right = g[some, :, :, :, cols].reshape(2 * NR * ROWS, TILE)
            total = lax.dot_general(
                left, right, (((0,), (0,)), ((), ())), preferred_element_type=F32
            )
            if part == 0:
                acc[:, cols] = total
            else:
                wg[:, cols] = (acc[:, cols] + total).astype(BF16)
            return carry

        lax.fori_loop(0, hidden // TILE, body, 0)

    def product(s, n):
        chunks = []
        for j in CUTS[PIECES[s]][n]:
            chunks += [(0, 0)] if j == 0 else [(4, 7)] if j == 4 else [(-j, 2 * j - 1), (j, 2 * j)]
        m2_part(s, chunks)

    outs = [
        pltpu.make_async_copy(a_v, b_v, out_sem.at[n])
        for n, (a_v, b_v) in enumerate(((act, act_ref), (wg, wg_ref), (ig, ig_ref)))
    ]

    def start_wgrad(part):
        wgrad(part)
        if part == 1:
            outs[0].start()
            outs[1].start()

    step = {"O": own, "F": forward, "M": m1, "R4": r4, "R3": r3, "R0": r0, "A4": a4, "P": pass_on, "FIN": fin, "WG": start_wgrad}
    for j in (1, 2):
        step[f"R{j}"] = functools.partial(lambda j, s: rj(s, j), j)
    for j in (1, 2, 3):
        step[f"A{j}"] = functools.partial(lambda j, s: a(s, j), j)
    for n in range(4):
        step[f"N{n}"] = functools.partial(lambda n, s: product(s, n), n)
    for name, s in ORDER:
        step[name](s)
    outs[2].start()

    for s in range(stages):
        wait_for(tok.at[s, pl.ds(0, NC - 1)], ag1_send.at[s])
        wait_for(px.at[s], px_send.at[s])
        wait_for(s4.at[s, :, lo], rs_send.at[s, 0])
        wait_for(s4.at[s, :, hi], rs_send.at[s, 1])
        for j in range(2, 8):
            wait_for(s4.at[s], rs_send.at[s, j])
        for j in range(6):
            wait_for(s4.at[s], ag_send.at[s, j])
        wait_for(s4.at[s, :, lo], ag_send.at[s, 6])
        wait_for(s4.at[s, :, hi], ag_send.at[s, 7])
        wait_for(g.at[s, :, 0], pt_send.at[s])
        if TWO[s]:
            wait_for(r2.at[s, pl.ds(0, 12)], r2_send.at[s])
            wait_for(r2.at[s, pl.ds(12, 3)], r2b_send.at[s])
        else:
            wait_for(r2.at[s], r2_send.at[s])
    for cp in outs:
        cp.wait()


def copy_kernel(*refs):
    copies = [pltpu.make_async_copy(refs[n], refs[3 + n], refs[6].at[n]) for n in range(3)]
    for cp in copies:
        cp.start()
    for cp in copies:
        cp.wait()


def kern(tokens, weight, cotangent):
    rows, width = tokens.shape
    hidden = weight.shape[1]
    stages = rows // ROWS
    vmem, dma = pltpu.VMEM, pltpu.SemaphoreType.DMA
    any_spec = pl.BlockSpec(memory_space=pl.ANY)
    return pl.pallas_call(
        functools.partial(kernel, stages),
        out_shape=(
            jax.ShapeDtypeStruct((rows, hidden), BF16),
            jax.ShapeDtypeStruct((rows, width), BF16),
            jax.ShapeDtypeStruct((width, hidden), BF16),
        ),
        in_specs=[any_spec] * 3,
        out_specs=(any_spec,) * 3,
        scratch_shapes=[
            vmem((width, hidden), BF16),
            vmem((rows, hidden), BF16),
            vmem((stages, NC, ROWS, width), BF16),
            vmem((stages, NZ, 2, ROWS, hidden), BF16),
            vmem((stages, NZ, ROWS, hidden), BF16),
            vmem((stages, ROWS, hidden), BF16),
            vmem((stages, 4, ROWS, hidden), BF16),
            vmem((stages, 4, ROWS, hidden), BF16),
            vmem((stages, 4, ROWS, hidden), BF16),
            vmem((stages, 4, ROWS, hidden), BF16),
            vmem((stages, NZ, 2, ROWS, hidden), BF16),
            vmem((stages, NC, ROWS, width), BF16),
            vmem((stages, NC - 1, ROWS, width), BF16),
            vmem((stages, ROWS, width), F32),
            vmem((stages, 3, ROWS, width), BF16),
            vmem((rows, hidden), BF16),
            vmem((rows, width), BF16),
            vmem((width, hidden), BF16),
            vmem((width, hidden), F32),
            dma((2 + stages,)), dma((3,)),
            dma((stages,)), dma((stages, 3)), dma((stages,)), dma((stages,)), dma((stages,)),
            dma((stages, 8)), dma((stages, 4)), dma((stages, 4)),
            dma((stages, 8)), dma((stages, 4)), dma((stages, 4)),
            dma((stages,)), dma((stages, 8)),
            dma((stages,)), dma((stages,)), dma((stages,)), dma((stages,)),
        ],
        compiler_params=pltpu.CompilerParams(
            collective_id=0, has_side_effects=True, vmem_limit_bytes=50 * 2**20
        ),
        name="updown",
    )(tokens, weight, cotangent)


def on_device(tokens, weight, cotangent):
    outs = kern(tokens, weight, cotangent)
    any_spec, dma = pl.BlockSpec(memory_space=pl.ANY), pltpu.SemaphoreType.DMA
    return tuple(pl.pallas_call(
        copy_kernel,
        out_shape=tuple(jax.ShapeDtypeStruct(o.shape, o.dtype) for o in outs),
        in_specs=[any_spec] * 3,
        out_specs=(any_spec,) * 3,
        scratch_shapes=[dma((3,))],
        compiler_params=pltpu.CompilerParams(vmem_limit_bytes=16 * 2**20),
        name="leave",
    )(*outs))


def solution(mesh):
    return jax.shard_map(
        on_device,
        mesh=mesh,
        in_specs=(P("col", "row"), P("row", "col"), P("row", "col")),
        out_specs=(P("row", "col"), P("col", "row"), P("row", "col")),
        check_vma=False,
    )
```

```python
import functools
import math

import jax
import jax.numpy as jnp
from jax import lax
from jax.experimental import pallas as pl
from jax.experimental.pallas import tpu as pltpu
from jax.sharding import PartitionSpec as P

MESH = pl.DeviceIdType.MESH
BF16 = jnp.bfloat16
F32 = jnp.float32

NR = 16
NC = 16
NZ = NR // 2
ROWS = 16
TILE = 512

CUTS = {
    1: ((0, 1, 2, 3, 4),), 2: ((0, 1, 2), (3, 4)), 3: ((0, 1, 2), (3,), (4,)), 4: ((0, 1), (2,), (3,), (4,)),
    5: ((0, 1, 2, 3), (4,)), 6: ((0, 1), (2, 3, 4)), 7: ((0, 1), (2, 3), (4,)),
}
NEED = (4, 3, -3, 2, -2, 1, -1, 0)
PIECES = (2, 2, 2, 3)
TWO = (1, 1, 1, 1)
DIRECT = (0, 0, 0, 0)
ORDER = (
    ("O", 0), ("O", 1), ("O", 2), ("O", 3), ("F", 0), ("F", 1), ("F", 2), ("F", 3), ("M", 0), ("M", 1),
    ("R4", 0), ("M", 2), ("R4", 1), ("M", 3), ("R3", 0), ("R4", 2), ("R3", 1), ("R4", 3), ("R2", 0), ("R3", 2),
    ("R2", 1), ("R3", 3), ("R1", 0), ("R2", 2), ("R1", 1), ("R2", 3), ("R0", 0), ("R1", 2), ("R0", 1),
    ("R1", 3), ("A1", 0), ("R0", 2), ("A1", 1), ("R0", 3), ("A2", 0), ("A1", 2), ("A2", 1), ("N0", 0),
    ("A1", 3), ("N0", 1), ("A3", 0), ("A2", 2), ("A3", 1), ("A2", 3), ("N0", 2), ("A4", 0), ("N0", 3),
    ("A3", 2), ("A4", 1), ("N1", 0), ("A3", 3), ("N1", 1), ("N1", 3), ("A4", 2), ("WG", 0), ("A4", 3),
    ("N1", 2), ("P", 0), ("N2", 3), ("P", 1), ("P", 2), ("P", 3), ("WG", 1), ("FIN", 0), ("FIN", 1), ("FIN", 2),
    ("FIN", 3),
)


def gelu_pair(value):
    phi = 0.5 * (1.0 + lax.erf(value * (1.0 / math.sqrt(2.0))))
    slope = phi + value * jnp.exp(-0.5 * value * value) * (1.0 / math.sqrt(2.0 * math.pi))
    return value * phi, slope


def kernel(
    stages,
    tok_ref, w_ref, cot_ref,
    act_ref, ig_ref, wg_ref,
    w, cot, tok, pp, px, s4, sp, sm, rp, rm, g, ip, r2, t0, t1, act, ig, wg, acc,
    in_sem, out_sem,
    ag1_send, ag1a_recv, ag1b_recv, px_send, px_recv,
    rs_send, rp_recv, rm_recv,
    ag_send, gp_recv, gm_recv, pt_send, pt_recv,
    r2_send, r2_recv, r2b_send, r2b_recv,
):
    r, c = lax.axis_index("row"), lax.axis_index("col")
    z, k = r // 2, lax.rem(r, 2)
    other = 1 - k
    width, hidden = w.shape
    half = hidden // 2
    lo, hi = pl.ds(0, half), pl.ds(half, half)

    up = (lax.rem(r + 2, NR), c)
    down = (lax.rem(r + NR - 2, NR), c)
    partner = (r + 1 - 2 * k, c)

    def peer(i):
        return lax.rem(c + i, NC)

    def shift(da, db):
        dx, dy = da + k * (db - da), db + k * (da - db)
        return lax.rem(c // 4 + dy + 4, 4) * 4 + lax.rem(c + dx + 4, 4)

    def offsets(dest):
        dx = lax.rem(lax.rem(dest, 4) - lax.rem(c, 4) + 4, 4)
        dy = lax.rem(dest // 4 - c // 4 + 4, 4)
        return dx + k * (dy - dx), dy + k * (dx - dy)

    def at_z(q):
        return lax.rem(z + q + NZ, NZ)

    def remote(src, dst, ss, rs, dev):
        cp = pltpu.make_async_remote_copy(
            src_ref=src, dst_ref=dst, send_sem=ss, recv_sem=rs,
            device_id=dev, device_id_type=MESH,
        )
        cp.start()

    def wait_for(ref, sem):
        pltpu.make_async_copy(ref, ref, sem).wait()

    loads = [
        pltpu.make_async_copy(w_ref, w, in_sem.at[0]),
        pltpu.make_async_copy(cot_ref, cot, in_sem.at[1]),
    ]
    for cp in loads:
        cp.start()

    barrier = pltpu.get_barrier_semaphore()
    if any(DIRECT) or not all(TWO):
        greeted = [(r, peer(i)) for i in range(1, NC)]
    else:
        greeted = [(r, shift(i, 0)) for i in (1, 2, 3)] + [(r, shift(0, i)) for i in (1, 2, 3)]
    greeted += [up, down, partner]
    for dev in greeted:
        pl.semaphore_signal(barrier, inc=1, device_id=dev, device_id_type=MESH)
    pl.semaphore_wait(barrier, len(greeted))

    own_copies = {}

    def own(s):
        block = tok_ref.at[pl.ds(s * ROWS, ROWS)]
        if DIRECT[s]:
            for i in range(1, NC):
                remote(block, tok.at[s, c], ag1_send.at[s], ag1b_recv.at[s], (r, peer(i)))
        else:
            for i in (1, 3, 2):
                remote(block, tok.at[s, c], ag1_send.at[s], ag1a_recv.at[s, i - 1], (r, shift(i, 0)))
            for i in (1, 3, 2):
                remote(block, tok.at[s, c], ag1_send.at[s], ag1b_recv.at[s], (r, shift(0, i)))
        cp = pltpu.make_async_copy(block, tok.at[s, c], in_sem.at[2 + s])
        cp.start()
        own_copies[s] = cp

    def forward(s):
        for i in (1, 3, 2):
            block = tok.at[s, shift(-i, 0)]
            wait_for(block, ag1a_recv.at[s, i - 1])
            for j in (1, 3, 2):
                remote(block, block, ag1_send.at[s], ag1b_recv.at[s], (r, shift(0, j)))

    def m1(s):
        if s == 0:
            loads[0].wait()
        own_copies[s].wait()
        wait_for(tok.at[s, pl.ds(0, 15 if DIRECT[s] else 12)], ag1b_recv.at[s])
        left = tok[s].reshape(NC * ROWS, width)
        part = jnp.dot(left, w[...], preferred_element_type=F32).astype(BF16)
        pp[s] = part.reshape(NZ, 2, ROWS, hidden)
        for q in NEED:
            d = at_z(q)
            remote(pp.at[s, d, other], px.at[s, d], px_send.at[s], px_recv.at[s, abs(q)], partner)

    def base(s, d):
        return pp[s, d, k].astype(F32) + px[s, d].astype(F32)

    def r4(s):
        wait_for(px.at[s, 0], px_recv.at[s, 4])
        s4[s] = base(s, at_z(4)).astype(BF16)
        remote(s4.at[s, :, lo], rp.at[s, 3, :, lo], rs_send.at[s, 0], rp_recv.at[s, 3], up)
        remote(s4.at[s, :, hi], rm.at[s, 3, :, hi], rs_send.at[s, 1], rm_recv.at[s, 3], down)

    def r3(s):
        wait_for(px.at[s, pl.ds(0, 2)], px_recv.at[s, 3])
        wait_for(rp.at[s, 3, :, lo], rp_recv.at[s, 3])
        up_sum = base(s, at_z(3))
        sp[s, 3, :, lo] = (up_sum[:, :half] + rp[s, 3, :, lo].astype(F32)).astype(BF16)
        sp[s, 3, :, hi] = up_sum[:, half:].astype(BF16)
        remote(sp.at[s, 3], rp.at[s, 2], rs_send.at[s, 2], rp_recv.at[s, 2], up)
        wait_for(rm.at[s, 3, :, hi], rm_recv.at[s, 3])
        down_sum = base(s, at_z(-3))
        sm[s, 3, :, hi] = (down_sum[:, half:] + rm[s, 3, :, hi].astype(F32)).astype(BF16)
        sm[s, 3, :, lo] = down_sum[:, :half].astype(BF16)
        remote(sm.at[s, 3], rm.at[s, 2], rs_send.at[s, 3], rm_recv.at[s, 2], down)

    def rj(s, j):
        wait_for(px.at[s, pl.ds(0, 2)], px_recv.at[s, j])
        wait_for(rp.at[s, j], rp_recv.at[s, j])
        sp[s, j] = (base(s, at_z(j)) + rp[s, j].astype(F32)).astype(BF16)
        remote(sp.at[s, j], rp.at[s, j - 1], rs_send.at[s, 8 - 2 * j], rp_recv.at[s, j - 1], up)
        wait_for(rm.at[s, j], rm_recv.at[s, j])
        sm[s, j] = (base(s, at_z(-j)) + rm[s, j].astype(F32)).astype(BF16)
        remote(sm.at[s, j], rm.at[s, j - 1], rs_send.at[s, 9 - 2 * j], rm_recv.at[s, j - 1], down)

    def r0(s):
        wait_for(px.at[s, 0], px_recv.at[s, 0])
        wait_for(rp.at[s, 0], rp_recv.at[s, 0])
        wait_for(rm.at[s, 0], rm_recv.at[s, 0])
        if s == 0:
            loads[1].wait()
        rows = pl.ds(s * ROWS, ROWS)
        pre = base(s, z) + rp[s, 0].astype(F32) + rm[s, 0].astype(F32)
        activated, slope = gelu_pair(pre)
        g[s, z, k] = (cot[rows].astype(F32) * slope).astype(BF16)
        mine = g.at[s, z, k]
        remote(mine, mine, ag_send.at[s, 0], gp_recv.at[s, 0], up)
        remote(mine, mine, ag_send.at[s, 1], gm_recv.at[s, 0], down)
        remote(mine, mine, pt_send.at[s], pt_recv.at[s, 0], partner)
        act[rows] = activated.astype(BF16)

    def a(s, j):
        below, above = g.at[s, at_z(-j), k], g.at[s, at_z(j), k]
        if j < 3:
            wait_for(below, gp_recv.at[s, j - 1])
            remote(below, below, ag_send.at[s, 2 * j], gp_recv.at[s, j], up)
            wait_for(above, gm_recv.at[s, j - 1])
            remote(above, above, ag_send.at[s, 2 * j + 1], gm_recv.at[s, j], down)
        else:
            wait_for(below, gp_recv.at[s, j - 1])
            part = g.at[s, at_z(-j), k, :, lo]
            remote(part, part, ag_send.at[s, 2 * j], gp_recv.at[s, j], up)
            wait_for(above, gm_recv.at[s, j - 1])
            part = g.at[s, at_z(j), k, :, hi]
            remote(part, part, ag_send.at[s, 2 * j + 1], gm_recv.at[s, j], down)
        remote(below, below, pt_send.at[s], pt_recv.at[s, 2 * j - 1], partner)
        remote(above, above, pt_send.at[s], pt_recv.at[s, 2 * j], partner)

    def a4(s):
        far = g.at[s, at_z(4), k]
        wait_for(g.at[s, at_z(4), k, :, lo], gp_recv.at[s, 3])
        wait_for(g.at[s, at_z(4), k, :, hi], gm_recv.at[s, 3])
        remote(far, far, pt_send.at[s], pt_recv.at[s, 7], partner)

    def pass_on(s):
        wait_for(r2.at[s, pl.ds(0, 12)], r2_recv.at[s])
        for j in (1, 3, 2, 0):
            total = ip[s, shift(0, j)].astype(F32)
            for i in range(3):
                total += r2[s, 4 * i + j].astype(F32)
            if j == 0:
                t0[s] = total
            else:
                t1[s, j - 1] = total.astype(BF16)
                remote(t1.at[s, j - 1], r2.at[s, 11 + j], r2b_send.at[s], r2b_recv.at[s], (r, shift(0, j)))

    def m2_part(s, chunks):
        for q, slot in chunks:
            wait_for(g.at[s, 0, 0], pt_recv.at[s, slot])
        if len(chunks) == NZ:
            left = g[s].reshape(NR * ROWS, hidden)
        else:
            left = jnp.concatenate(
                [g[s, at_z(q)].reshape(2 * ROWS, hidden) for q, _ in chunks], axis=0
            )
        part = lax.dot_general(
            left, w[...], (((1,), (1,)), ((), ())), preferred_element_type=F32
        ).astype(BF16)
        part = part.reshape(len(chunks), 2, ROWS, width)
        if len(chunks) == NZ:
            ip[s] = part.reshape(NC, ROWS, width)
        for n, (q, _) in enumerate(chunks):
            d = at_z(q)
            if len(chunks) < NZ:
                ip[s, pl.ds(2 * d, 2)] = part[n]
            for m in range(2):
                dest = 2 * d + m
                if TWO[s]:
                    i, j = offsets(dest)

                    @pl.when(i != 0)
                    def _():
                        slot = 4 * i - 4 + j
                        remote(ip.at[s, dest], r2.at[s, slot], r2_send.at[s], r2_recv.at[s], (r, shift(i, 0)))
                else:

                    @pl.when(dest != c)
                    def _():
                        slot = lax.rem(dest - c + NC, NC) - 1
                        remote(ip.at[s, dest], r2.at[s, slot], r2_send.at[s], r2_recv.at[s], (r, dest))

    def fin(s):
        if TWO[s]:
            wait_for(r2.at[s, pl.ds(12, 3)], r2b_recv.at[s])
            total = t0[s]
            for j in range(3):
                total += r2[s, 12 + j].astype(F32)
            ig[pl.ds(s * ROWS, ROWS)] = total.astype(BF16)
            return
        wait_for(r2.at[s], r2_recv.at[s])
        total = ip[s, c].astype(F32)
        for i in range(NC - 1):
            total += r2[s, i].astype(F32)
        ig[pl.ds(s * ROWS, ROWS)] = total.astype(BF16)

    def wgrad(part):
        some = pl.ds(2 * part, 2)

        def body(j, carry):
            cols = pl.ds(pl.multiple_of(j * TILE, TILE), TILE)
            left = tok[some].reshape(2 * NC * ROWS, width)
            right = g[some, :, :, :, cols].reshape(2 * NR * ROWS, TILE)
            total = lax.dot_general(
                left, right, (((0,), (0,)), ((), ())), preferred_element_type=F32
            )
            if part == 0:
                acc[:, cols] = total
            else:
                wg[:, cols] = (acc[:, cols] + total).astype(BF16)
            return carry

        lax.fori_loop(0, hidden // TILE, body, 0)

    def product(s, n):
        chunks = []
        for j in CUTS[PIECES[s]][n]:
            chunks += [(0, 0)] if j == 0 else [(4, 7)] if j == 4 else [(-j, 2 * j - 1), (j, 2 * j)]
        m2_part(s, chunks)

    outs = [
        pltpu.make_async_copy(a_v, b_v, out_sem.at[n])
        for n, (a_v, b_v) in enumerate(((act, act_ref), (wg, wg_ref), (ig, ig_ref)))
    ]

    def start_wgrad(part):
        wgrad(part)
        if part == 1:
            outs[0].start()
            outs[1].start()

    step = {"O": own, "F": forward, "M": m1, "R4": r4, "R3": r3, "R0": r0, "A4": a4, "P": pass_on, "FIN": fin, "WG": start_wgrad}
    for j in (1, 2):
        step[f"R{j}"] = functools.partial(lambda j, s: rj(s, j), j)
    for j in (1, 2, 3):
        step[f"A{j}"] = functools.partial(lambda j, s: a(s, j), j)
    for n in range(4):
        step[f"N{n}"] = functools.partial(lambda n, s: product(s, n), n)
    for name, s in ORDER:
        step[name](s)
    outs[2].start()

    for s in range(stages):
        wait_for(tok.at[s, pl.ds(0, NC - 1)], ag1_send.at[s])
        wait_for(px.at[s], px_send.at[s])
        wait_for(s4.at[s, :, lo], rs_send.at[s, 0])
        wait_for(s4.at[s, :, hi], rs_send.at[s, 1])
        for j in range(2, 8):
            wait_for(s4.at[s], rs_send.at[s, j])
        for j in range(6):
            wait_for(s4.at[s], ag_send.at[s, j])
        wait_for(s4.at[s, :, lo], ag_send.at[s, 6])
        wait_for(s4.at[s, :, hi], ag_send.at[s, 7])
        wait_for(g.at[s, :, 0], pt_send.at[s])
        if TWO[s]:
            wait_for(r2.at[s, pl.ds(0, 12)], r2_send.at[s])
            wait_for(r2.at[s, pl.ds(12, 3)], r2b_send.at[s])
        else:
            wait_for(r2.at[s], r2_send.at[s])
    for cp in outs:
        cp.wait()


def copy_kernel(*refs):
    copies = [pltpu.make_async_copy(refs[n], refs[3 + n], refs[6].at[n]) for n in range(3)]
    for cp in copies:
        cp.start()
    for cp in copies:
        cp.wait()


def kern(tokens, weight, cotangent):
    rows, width = tokens.shape
    hidden = weight.shape[1]
    stages = rows // ROWS
    vmem, dma = pltpu.VMEM, pltpu.SemaphoreType.DMA
    any_spec = pl.BlockSpec(memory_space=pl.ANY)
    return pl.pallas_call(
        functools.partial(kernel, stages),
        out_shape=(
            jax.ShapeDtypeStruct((rows, hidden), BF16),
            jax.ShapeDtypeStruct((rows, width), BF16),
            jax.ShapeDtypeStruct((width, hidden), BF16),
        ),
        in_specs=[any_spec] * 3,
        out_specs=(any_spec,) * 3,
        scratch_shapes=[
            vmem((width, hidden), BF16),
            vmem((rows, hidden), BF16),
            vmem((stages, NC, ROWS, width), BF16),
            vmem((stages, NZ, 2, ROWS, hidden), BF16),
            vmem((stages, NZ, ROWS, hidden), BF16),
            vmem((stages, ROWS, hidden), BF16),
            vmem((stages, 4, ROWS, hidden), BF16),
            vmem((stages, 4, ROWS, hidden), BF16),
            vmem((stages, 4, ROWS, hidden), BF16),
            vmem((stages, 4, ROWS, hidden), BF16),
            vmem((stages, NZ, 2, ROWS, hidden), BF16),
            vmem((stages, NC, ROWS, width), BF16),
            vmem((stages, NC - 1, ROWS, width), BF16),
            vmem((stages, ROWS, width), F32),
            vmem((stages, 3, ROWS, width), BF16),
            vmem((rows, hidden), BF16),
            vmem((rows, width), BF16),
            vmem((width, hidden), BF16),
            vmem((width, hidden), F32),
            dma((2 + stages,)), dma((3,)),
            dma((stages,)), dma((stages, 3)), dma((stages,)), dma((stages,)), dma((stages, 5)),
            dma((stages, 8)), dma((stages, 4)), dma((stages, 4)),
            dma((stages, 8)), dma((stages, 4)), dma((stages, 4)),
            dma((stages,)), dma((stages, 8)),
            dma((stages,)), dma((stages,)), dma((stages,)), dma((stages,)),
        ],
        compiler_params=pltpu.CompilerParams(
            collective_id=0, has_side_effects=True, vmem_limit_bytes=50 * 2**20
        ),
        name="updown",
    )(tokens, weight, cotangent)


def on_device(tokens, weight, cotangent):
    tokens, weight, cotangent = (
        pltpu.with_memory_space_constraint(v, pltpu.HBM) for v in (tokens, weight, cotangent)
    )
    outs = kern(tokens, weight, cotangent)
    any_spec, dma = pl.BlockSpec(memory_space=pl.ANY), pltpu.SemaphoreType.DMA
    return tuple(pl.pallas_call(
        copy_kernel,
        out_shape=tuple(jax.ShapeDtypeStruct(o.shape, o.dtype) for o in outs),
        in_specs=[any_spec] * 3,
        out_specs=(any_spec,) * 3,
        scratch_shapes=[dma((3,))],
        compiler_params=pltpu.CompilerParams(vmem_limit_bytes=16 * 2**20),
        name="leave",
    )(*outs))


def solution(mesh):
    return jax.shard_map(
        on_device,
        mesh=mesh,
        in_specs=(P("col", "row"), P("row", "col"), P("row", "col")),
        out_specs=(P("row", "col"), P("col", "row"), P("row", "col")),
        check_vma=False,
    )
```

```python
import functools
import math

import jax
import jax.numpy as jnp
from jax import lax
from jax.experimental import pallas as pl
from jax.experimental.pallas import tpu as pltpu
from jax.sharding import PartitionSpec as P

MESH = pl.DeviceIdType.MESH
BF16 = jnp.bfloat16
F32 = jnp.float32

NR = 16
NC = 16
NZ = NR // 2
ROWS = 16
TILE = 512

CUTS = {
    1: ((0, 1, 2, 3, 4),), 2: ((0, 1, 2), (3, 4)), 3: ((0, 1, 2), (3,), (4,)), 4: ((0, 1), (2,), (3,), (4,)),
    5: ((0, 1, 2, 3), (4,)), 6: ((0, 1), (2, 3, 4)), 7: ((0, 1), (2, 3), (4,)),
}
NEED = (4, 3, -3, 2, -2, 1, -1, 0)
PIECES = (2, 2, 2, 3)
TWO = (1, 1, 1, 1)
DIRECT = (0, 0, 0, 0)
ORDER = (
    ("O", 0), ("O", 1), ("O", 2), ("O", 3), ("F", 0), ("F", 1), ("F", 2), ("F", 3), ("M", 0), ("R4", 0),
    ("M", 1), ("R4", 1), ("R3", 0), ("M", 2), ("R4", 2), ("R3", 1), ("M", 3), ("R4", 3), ("R2", 0), ("R3", 2),
    ("R2", 1), ("R3", 3), ("R1", 0), ("R2", 2), ("R1", 1), ("R2", 3), ("R0", 0), ("R1", 2), ("R0", 1),
    ("R1", 3), ("A1", 0), ("R0", 2), ("A1", 1), ("R0", 3), ("A2", 0), ("A1", 2), ("A2", 1), ("N0", 0),
    ("A1", 3), ("N0", 1), ("A3", 0), ("A2", 2), ("A3", 1), ("A2", 3), ("N0", 2), ("A4", 0), ("N0", 3),
    ("A3", 2), ("A4", 1), ("N1", 0), ("A3", 3), ("N1", 1), ("N1", 3), ("A4", 2), ("A4", 3), ("N1", 2),
    ("N2", 3), ("P", 0), ("P", 1), ("WG", 0), ("P", 2), ("P", 3), ("WG", 1), ("W", 0), ("FIN", 0), ("FIN", 1),
    ("FIN", 2), ("FIN", 3),
)


def gelu_pair(value):
    phi = 0.5 * (1.0 + lax.erf(value * (1.0 / math.sqrt(2.0))))
    slope = phi + value * jnp.exp(-0.5 * value * value) * (1.0 / math.sqrt(2.0 * math.pi))
    return value * phi, slope


def kernel(
    stages,
    tok_ref, w_ref, cot_ref,
    act_ref, ig_ref, wg_ref,
    w, cot, tok, pp, px, s4, sp, sm, rp, rm, g, ip, r2, t0, t1, act, ig, wg, acc,
    in_sem, out_sem,
    ag1_send, ag1a_recv, ag1b_recv, px_send, px_recv,
    rs_send, rp_recv, rm_recv,
    ag_send, gp_recv, gm_recv, pt_send, pt_recv,
    r2_send, r2_recv, r2b_send, r2b_recv,
):
    r, c = lax.axis_index("row"), lax.axis_index("col")
    z, k = r // 2, lax.rem(r, 2)
    other = 1 - k
    width, hidden = w.shape
    half = hidden // 2
    lo, hi = pl.ds(0, half), pl.ds(half, half)

    up = (lax.rem(r + 2, NR), c)
    down = (lax.rem(r + NR - 2, NR), c)
    partner = (r + 1 - 2 * k, c)

    def peer(i):
        return lax.rem(c + i, NC)

    def shift(da, db):
        dx, dy = da + k * (db - da), db + k * (da - db)
        return lax.rem(c // 4 + dy + 4, 4) * 4 + lax.rem(c + dx + 4, 4)

    def offsets(dest):
        dx = lax.rem(lax.rem(dest, 4) - lax.rem(c, 4) + 4, 4)
        dy = lax.rem(dest // 4 - c // 4 + 4, 4)
        return dx + k * (dy - dx), dy + k * (dx - dy)

    def at_z(q):
        return lax.rem(z + q + NZ, NZ)

    def remote(src, dst, ss, rs, dev):
        cp = pltpu.make_async_remote_copy(
            src_ref=src, dst_ref=dst, send_sem=ss, recv_sem=rs,
            device_id=dev, device_id_type=MESH,
        )
        cp.start()

    def wait_for(ref, sem):
        pltpu.make_async_copy(ref, ref, sem).wait()

    own_copies = [
        pltpu.make_async_copy(tok_ref.at[pl.ds(s * ROWS, ROWS)], tok.at[s, c], in_sem.at[2 + s])
        for s in range(stages)
    ]
    for cp in own_copies:
        cp.start()
    loads = [
        pltpu.make_async_copy(w_ref, w, in_sem.at[0]),
        pltpu.make_async_copy(cot_ref, cot, in_sem.at[1]),
    ]
    for cp in loads:
        cp.start()

    barrier = pltpu.get_barrier_semaphore()
    if any(DIRECT) or not all(TWO):
        greeted = [(r, peer(i)) for i in range(1, NC)]
    else:
        greeted = [(r, shift(i, 0)) for i in (1, 2, 3)] + [(r, shift(0, i)) for i in (1, 2, 3)]
    greeted += [up, down, partner]
    for dev in greeted:
        pl.semaphore_signal(barrier, inc=1, device_id=dev, device_id_type=MESH)
    pl.semaphore_wait(barrier, len(greeted))

    def own(s):
        own_copies[s].wait()
        block = tok.at[s, c]
        if DIRECT[s]:
            for i in range(1, NC):
                remote(block, tok.at[s, c], ag1_send.at[s], ag1b_recv.at[s], (r, peer(i)))
        else:
            for i in (2, 1, 3):
                remote(block, tok.at[s, c], ag1_send.at[s], ag1a_recv.at[s, i - 1], (r, shift(i, 0)))
            for i in (2, 1, 3):
                remote(block, tok.at[s, c], ag1_send.at[s], ag1b_recv.at[s], (r, shift(0, i)))

    def forward(s):
        for i in (2, 1, 3):
            block = tok.at[s, shift(-i, 0)]
            wait_for(block, ag1a_recv.at[s, i - 1])
            for j in (2, 1, 3):
                remote(block, block, ag1_send.at[s], ag1b_recv.at[s], (r, shift(0, j)))

    def m1(s):
        if s == 0:
            loads[0].wait()
        wait_for(tok.at[s, pl.ds(0, 15 if DIRECT[s] else 12)], ag1b_recv.at[s])
        left = tok[s].reshape(NC * ROWS, width)
        part = jnp.dot(left, w[...], preferred_element_type=F32).astype(BF16)
        pp[s] = part.reshape(NZ, 2, ROWS, hidden)
        for q in NEED:
            d = at_z(q)
            remote(pp.at[s, d, other], px.at[s, d], px_send.at[s], px_recv.at[s, abs(q)], partner)

    def base(s, d):
        return pp[s, d, k].astype(F32) + px[s, d].astype(F32)

    def r4(s):
        wait_for(px.at[s, 0], px_recv.at[s, 4])
        s4[s] = base(s, at_z(4)).astype(BF16)
        remote(s4.at[s, :, lo], rp.at[s, 3, :, lo], rs_send.at[s, 0], rp_recv.at[s, 3], up)
        remote(s4.at[s, :, hi], rm.at[s, 3, :, hi], rs_send.at[s, 1], rm_recv.at[s, 3], down)

    def r3(s):
        wait_for(px.at[s, pl.ds(0, 2)], px_recv.at[s, 3])
        wait_for(rp.at[s, 3, :, lo], rp_recv.at[s, 3])
        up_sum = base(s, at_z(3))
        sp[s, 3, :, lo] = (up_sum[:, :half] + rp[s, 3, :, lo].astype(F32)).astype(BF16)
        sp[s, 3, :, hi] = up_sum[:, half:].astype(BF16)
        remote(sp.at[s, 3], rp.at[s, 2], rs_send.at[s, 2], rp_recv.at[s, 2], up)
        wait_for(rm.at[s, 3, :, hi], rm_recv.at[s, 3])
        down_sum = base(s, at_z(-3))
        sm[s, 3, :, hi] = (down_sum[:, half:] + rm[s, 3, :, hi].astype(F32)).astype(BF16)
        sm[s, 3, :, lo] = down_sum[:, :half].astype(BF16)
        remote(sm.at[s, 3], rm.at[s, 2], rs_send.at[s, 3], rm_recv.at[s, 2], down)

    def rj(s, j):
        wait_for(px.at[s, pl.ds(0, 2)], px_recv.at[s, j])
        up_sum, down_sum = base(s, at_z(j)), base(s, at_z(-j))
        wait_for(rp.at[s, j], rp_recv.at[s, j])
        sp[s, j] = (up_sum + rp[s, j].astype(F32)).astype(BF16)
        remote(sp.at[s, j], rp.at[s, j - 1], rs_send.at[s, 8 - 2 * j], rp_recv.at[s, j - 1], up)
        wait_for(rm.at[s, j], rm_recv.at[s, j])
        sm[s, j] = (down_sum + rm[s, j].astype(F32)).astype(BF16)
        remote(sm.at[s, j], rm.at[s, j - 1], rs_send.at[s, 9 - 2 * j], rm_recv.at[s, j - 1], down)

    def r0(s):
        wait_for(px.at[s, 0], px_recv.at[s, 0])
        wait_for(rp.at[s, 0], rp_recv.at[s, 0])
        wait_for(rm.at[s, 0], rm_recv.at[s, 0])
        if s == 0:
            loads[1].wait()
        rows = pl.ds(s * ROWS, ROWS)
        pre = base(s, z) + rp[s, 0].astype(F32) + rm[s, 0].astype(F32)
        activated, slope = gelu_pair(pre)
        g[s, z, k] = (cot[rows].astype(F32) * slope).astype(BF16)
        mine = g.at[s, z, k]
        remote(mine, mine, ag_send.at[s, 0], gp_recv.at[s, 0], up)
        remote(mine, mine, ag_send.at[s, 1], gm_recv.at[s, 0], down)
        remote(mine, mine, pt_send.at[s], pt_recv.at[s, 0], partner)
        act[rows] = activated.astype(BF16)

    def a(s, j):
        below, above = g.at[s, at_z(-j), k], g.at[s, at_z(j), k]
        if j < 3:
            wait_for(below, gp_recv.at[s, j - 1])
            remote(below, below, ag_send.at[s, 2 * j], gp_recv.at[s, j], up)
            wait_for(above, gm_recv.at[s, j - 1])
            remote(above, above, ag_send.at[s, 2 * j + 1], gm_recv.at[s, j], down)
        else:
            wait_for(below, gp_recv.at[s, j - 1])
            part = g.at[s, at_z(-j), k, :, lo]
            remote(part, part, ag_send.at[s, 2 * j], gp_recv.at[s, j], up)
            wait_for(above, gm_recv.at[s, j - 1])
            part = g.at[s, at_z(j), k, :, hi]
            remote(part, part, ag_send.at[s, 2 * j + 1], gm_recv.at[s, j], down)
        remote(below, below, pt_send.at[s], pt_recv.at[s, 2 * j - 1], partner)
        remote(above, above, pt_send.at[s], pt_recv.at[s, 2 * j], partner)

    def a4(s):
        far = g.at[s, at_z(4), k]
        wait_for(g.at[s, at_z(4), k, :, lo], gp_recv.at[s, 3])
        wait_for(g.at[s, at_z(4), k, :, hi], gm_recv.at[s, 3])
        remote(far, far, pt_send.at[s], pt_recv.at[s, 7], partner)

    def pass_on(s):
        wait_for(r2.at[s, pl.ds(0, 12)], r2_recv.at[s])
        for j in (2, 1, 3, 0):
            total = ip[s, shift(0, j)].astype(F32)
            for i in range(3):
                total += r2[s, 4 * i + j].astype(F32)
            if j == 0:
                t0[s] = total
            else:
                t1[s, j - 1] = total.astype(BF16)
                remote(t1.at[s, j - 1], r2.at[s, 11 + j], r2b_send.at[s], r2b_recv.at[s], (r, shift(0, j)))

    def m2_part(s, chunks):
        for q, slot in chunks:
            wait_for(g.at[s, 0, 0], pt_recv.at[s, slot])
        if len(chunks) == NZ:
            left = g[s].reshape(NR * ROWS, hidden)
        else:
            left = jnp.concatenate(
                [g[s, at_z(q)].reshape(2 * ROWS, hidden) for q, _ in chunks], axis=0
            )
        part = lax.dot_general(
            left, w[...], (((1,), (1,)), ((), ())), preferred_element_type=F32
        ).astype(BF16)
        part = part.reshape(len(chunks), 2, ROWS, width)
        if len(chunks) == NZ:
            ip[s] = part.reshape(NC, ROWS, width)
        for n, (q, _) in enumerate(chunks):
            d = at_z(q)
            if len(chunks) < NZ:
                ip[s, pl.ds(2 * d, 2)] = part[n]
            for m in range(2):
                dest = 2 * d + m
                if TWO[s]:
                    i, j = offsets(dest)

                    @pl.when(i != 0)
                    def _():
                        slot = 4 * i - 4 + j
                        remote(ip.at[s, dest], r2.at[s, slot], r2_send.at[s], r2_recv.at[s], (r, shift(i, 0)))
                else:

                    @pl.when(dest != c)
                    def _():
                        slot = lax.rem(dest - c + NC, NC) - 1
                        remote(ip.at[s, dest], r2.at[s, slot], r2_send.at[s], r2_recv.at[s], (r, dest))

    def fin(s):
        if TWO[s]:
            wait_for(r2.at[s, pl.ds(12, 3)], r2b_recv.at[s])
            total = t0[s]
            for j in range(3):
                total += r2[s, 12 + j].astype(F32)
            ig[pl.ds(s * ROWS, ROWS)] = total.astype(BF16)
            return
        wait_for(r2.at[s], r2_recv.at[s])
        total = ip[s, c].astype(F32)
        for i in range(NC - 1):
            total += r2[s, i].astype(F32)
        ig[pl.ds(s * ROWS, ROWS)] = total.astype(BF16)

    def wgrad(part):
        some = pl.ds(2 * part, 2)

        def body(j, carry):
            cols = pl.ds(pl.multiple_of(j * TILE, TILE), TILE)
            left = tok[some].reshape(2 * NC * ROWS, width)
            right = g[some, :, :, :, cols].reshape(2 * NR * ROWS, TILE)
            total = lax.dot_general(
                left, right, (((0,), (0,)), ((), ())), preferred_element_type=F32
            )
            if part == 0:
                acc[:, cols] = total
            else:
                wg[:, cols] = (acc[:, cols] + total).astype(BF16)
            return carry

        lax.fori_loop(0, hidden // TILE, body, 0)

    def product(s, n):
        chunks = []
        for j in CUTS[PIECES[s]][n]:
            chunks += [(0, 0)] if j == 0 else [(4, 7)] if j == 4 else [(-j, 2 * j - 1), (j, 2 * j)]
        m2_part(s, chunks)

    outs = [
        pltpu.make_async_copy(a_v, b_v, out_sem.at[n])
        for n, (a_v, b_v) in enumerate(((act, act_ref), (wg, wg_ref), (ig, ig_ref)))
    ]

    def start_wgrad(part):
        wgrad(part)
        if part == 1:
            outs[0].start()
            outs[1].start()

    def settle(_):
        for s in range(stages):
            wait_for(tok.at[s, pl.ds(0, NC - 1)], ag1_send.at[s])
            wait_for(px.at[s], px_send.at[s])
            wait_for(s4.at[s, :, lo], rs_send.at[s, 0])
            wait_for(s4.at[s, :, hi], rs_send.at[s, 1])
            for j in range(2, 8):
                wait_for(s4.at[s], rs_send.at[s, j])
            for j in range(6):
                wait_for(s4.at[s], ag_send.at[s, j])
            wait_for(s4.at[s, :, lo], ag_send.at[s, 6])
            wait_for(s4.at[s, :, hi], ag_send.at[s, 7])
            wait_for(g.at[s, :, 0], pt_send.at[s])
            if TWO[s]:
                wait_for(r2.at[s, pl.ds(0, 12)], r2_send.at[s])

    step = {"O": own, "F": forward, "M": m1, "R4": r4, "R3": r3, "R0": r0, "A4": a4, "P": pass_on, "FIN": fin, "WG": start_wgrad, "W": settle}
    for j in (1, 2):
        step[f"R{j}"] = functools.partial(lambda j, s: rj(s, j), j)
    for j in (1, 2, 3):
        step[f"A{j}"] = functools.partial(lambda j, s: a(s, j), j)
    for n in range(4):
        step[f"N{n}"] = functools.partial(lambda n, s: product(s, n), n)
    for name, s in ORDER:
        step[name](s)
    outs[2].start()

    for s in range(stages):
        if TWO[s]:
            wait_for(r2.at[s, pl.ds(12, 3)], r2b_send.at[s])
        else:
            wait_for(r2.at[s], r2_send.at[s])
    for cp in outs:
        cp.wait()


def copy_kernel(*refs):
    copies = [pltpu.make_async_copy(refs[n], refs[3 + n], refs[6].at[n]) for n in range(3)]
    for cp in copies:
        cp.start()
    for cp in copies:
        cp.wait()


def kern(tokens, weight, cotangent):
    rows, width = tokens.shape
    hidden = weight.shape[1]
    stages = rows // ROWS
    vmem, dma = pltpu.VMEM, pltpu.SemaphoreType.DMA
    any_spec = pl.BlockSpec(memory_space=pl.ANY)
    return pl.pallas_call(
        functools.partial(kernel, stages),
        out_shape=(
            jax.ShapeDtypeStruct((rows, hidden), BF16),
            jax.ShapeDtypeStruct((rows, width), BF16),
            jax.ShapeDtypeStruct((width, hidden), BF16),
        ),
        in_specs=[any_spec] * 3,
        out_specs=(any_spec,) * 3,
        scratch_shapes=[
            vmem((width, hidden), BF16),
            vmem((rows, hidden), BF16),
            vmem((stages, NC, ROWS, width), BF16),
            vmem((stages, NZ, 2, ROWS, hidden), BF16),
            vmem((stages, NZ, ROWS, hidden), BF16),
            vmem((stages, ROWS, hidden), BF16),
            vmem((stages, 4, ROWS, hidden), BF16),
            vmem((stages, 4, ROWS, hidden), BF16),
            vmem((stages, 4, ROWS, hidden), BF16),
            vmem((stages, 4, ROWS, hidden), BF16),
            vmem((stages, NZ, 2, ROWS, hidden), BF16),
            vmem((stages, NC, ROWS, width), BF16),
            vmem((stages, NC - 1, ROWS, width), BF16),
            vmem((stages, ROWS, width), F32),
            vmem((stages, 3, ROWS, width), BF16),
            vmem((rows, hidden), BF16),
            vmem((rows, width), BF16),
            vmem((width, hidden), BF16),
            vmem((width, hidden), F32),
            dma((2 + stages,)), dma((3,)),
            dma((stages,)), dma((stages, 3)), dma((stages,)), dma((stages,)), dma((stages, 5)),
            dma((stages, 8)), dma((stages, 4)), dma((stages, 4)),
            dma((stages, 8)), dma((stages, 4)), dma((stages, 4)),
            dma((stages,)), dma((stages, 8)),
            dma((stages,)), dma((stages,)), dma((stages,)), dma((stages,)),
        ],
        compiler_params=pltpu.CompilerParams(
            collective_id=0, has_side_effects=True, vmem_limit_bytes=50 * 2**20
        ),
        name="updown",
    )(tokens, weight, cotangent)


def on_device(tokens, weight, cotangent):
    tokens, weight, cotangent = (
        pltpu.with_memory_space_constraint(v, pltpu.HBM) for v in (tokens, weight, cotangent)
    )
    outs = kern(tokens, weight, cotangent)
    any_spec, dma = pl.BlockSpec(memory_space=pl.ANY), pltpu.SemaphoreType.DMA
    return tuple(pl.pallas_call(
        copy_kernel,
        out_shape=tuple(jax.ShapeDtypeStruct(o.shape, o.dtype) for o in outs),
        in_specs=[any_spec] * 3,
        out_specs=(any_spec,) * 3,
        scratch_shapes=[dma((3,))],
        compiler_params=pltpu.CompilerParams(vmem_limit_bytes=16 * 2**20),
        name="leave",
    )(*outs))


def solution(mesh):
    return jax.shard_map(
        on_device,
        mesh=mesh,
        in_specs=(P("col", "row"), P("row", "col"), P("row", "col")),
        out_specs=(P("row", "col"), P("col", "row"), P("row", "col")),
        check_vma=False,
    )
```

```python
import functools
import math

import jax
import jax.numpy as jnp
from jax import lax
from jax.experimental import pallas as pl
from jax.experimental.pallas import tpu as pltpu
from jax.sharding import PartitionSpec as P

MESH = pl.DeviceIdType.MESH
BF16 = jnp.bfloat16
F32 = jnp.float32

NR = 16
NC = 16
NZ = NR // 2
ROWS = 16
TILE = 512

CUTS = {
    1: ((0, 1, 2, 3, 4),), 2: ((0, 1, 2), (3, 4)), 3: ((0, 1, 2), (3,), (4,)), 4: ((0, 1), (2,), (3,), (4,)),
    5: ((0, 1, 2, 3), (4,)), 6: ((0, 1), (2, 3, 4)), 7: ((0, 1), (2, 3), (4,)),
}
NEED = (4, 3, -3, 2, -2, 1, -1, 0)
PIECES = (2, 2, 2, 3)
TWO = (1, 1, 1, 1)
DIRECT = (0, 0, 0, 0)
ORDER = (
    ("O", 0), ("O", 1), ("O", 2), ("O", 3), ("F", 0), ("F", 1), ("F", 2), ("F", 3), ("M", 0), ("R4", 0),
    ("M", 1), ("R4", 1), ("R3", 0), ("M", 2), ("R4", 2), ("R3", 1), ("M", 3), ("R4", 3), ("R2", 0), ("R3", 2),
    ("R2", 1), ("R3", 3), ("R1", 0), ("R2", 2), ("R1", 1), ("R2", 3), ("R0", 0), ("R1", 2), ("R0", 1),
    ("R1", 3), ("A1", 0), ("R0", 2), ("A1", 1), ("R0", 3), ("A2", 0), ("A1", 2), ("A2", 1), ("N0", 0),
    ("A1", 3), ("N0", 1), ("A3", 0), ("A2", 2), ("A3", 1), ("A2", 3), ("N0", 2), ("A4", 0), ("N0", 3),
    ("A3", 2), ("A4", 1), ("N1", 0), ("A3", 3), ("N1", 1), ("N1", 3), ("A4", 2), ("A4", 3), ("N1", 2),
    ("N2", 3), ("P", 0), ("P", 1), ("WG", 0), ("P", 2), ("P", 3), ("WG", 1), ("W", 0), ("FIN", 0), ("FIN", 1),
    ("FIN", 2), ("FIN", 3),
)


def gelu_pair(value):
    phi = 0.5 * (1.0 + lax.erf(value * (1.0 / math.sqrt(2.0))))
    slope = phi + value * jnp.exp(-0.5 * value * value) * (1.0 / math.sqrt(2.0 * math.pi))
    return value * phi, slope


def kernel(
    stages,
    tok_ref, w_ref, cot_ref,
    act_ref, ig_ref, wg_ref,
    w, cot, tok, pp, px, s4, sp, sm, rp, rm, g, ip, r2, t0, t1, act, ig, wg, acc,
    in_sem, out_sem,
    ag1_send, ag1a_recv, ag1b_recv, px_send, px_recv,
    rs_send, rp_recv, rm_recv,
    ag_send, gp_recv, gm_recv, pt_send, pt_recv,
    r2_send, r2_recv, r2b_send, r2b_recv,
):
    r, c = lax.axis_index("row"), lax.axis_index("col")
    z, k = r // 2, lax.rem(r, 2)
    other = 1 - k
    width, hidden = w.shape
    half = hidden // 2
    lo, hi = pl.ds(0, half), pl.ds(half, half)

    up = (lax.rem(r + 2, NR), c)
    down = (lax.rem(r + NR - 2, NR), c)
    partner = (r + 1 - 2 * k, c)

    def peer(i):
        return lax.rem(c + i, NC)

    def shift(da, db):
        dx, dy = da + k * (db - da), db + k * (da - db)
        return lax.rem(c // 4 + dy + 4, 4) * 4 + lax.rem(c + dx + 4, 4)

    def offsets(dest):
        dx = lax.rem(lax.rem(dest, 4) - lax.rem(c, 4) + 4, 4)
        dy = lax.rem(dest // 4 - c // 4 + 4, 4)
        return dx + k * (dy - dx), dy + k * (dx - dy)

    def at_z(q):
        return lax.rem(z + q + NZ, NZ)

    def remote(src, dst, ss, rs, dev):
        cp = pltpu.make_async_remote_copy(
            src_ref=src, dst_ref=dst, send_sem=ss, recv_sem=rs,
            device_id=dev, device_id_type=MESH,
        )
        cp.start()

    def wait_for(ref, sem):
        pltpu.make_async_copy(ref, ref, sem).wait()

    own_copies = [
        pltpu.make_async_copy(tok_ref.at[pl.ds(s * ROWS, ROWS)], tok.at[s, c], in_sem.at[2 + s])
        for s in range(stages)
    ]
    for cp in own_copies:
        cp.start()
    loads = [
        pltpu.make_async_copy(w_ref, w, in_sem.at[0]),
        pltpu.make_async_copy(cot_ref, cot, in_sem.at[1]),
    ]
    for cp in loads:
        cp.start()

    barrier = pltpu.get_barrier_semaphore()
    if any(DIRECT) or not all(TWO):
        greeted = [(r, peer(i)) for i in range(1, NC)]
    else:
        greeted = [(r, shift(i, 0)) for i in (1, 2, 3)] + [(r, shift(0, i)) for i in (1, 2, 3)]
    greeted += [up, down, partner]
    for dev in greeted:
        pl.semaphore_signal(barrier, inc=1, device_id=dev, device_id_type=MESH)
    pl.semaphore_wait(barrier, len(greeted))

    def own(s):
        own_copies[s].wait()
        block = tok.at[s, c]
        if DIRECT[s]:
            for i in range(1, NC):
                remote(block, tok.at[s, c], ag1_send.at[s], ag1b_recv.at[s], (r, peer(i)))
        else:
            for i in (2, 1, 3):
                remote(block, tok.at[s, c], ag1_send.at[s], ag1a_recv.at[s, i - 1], (r, shift(i, 0)))
            for i in (2, 1, 3):
                remote(block, tok.at[s, c], ag1_send.at[s], ag1b_recv.at[s], (r, shift(0, i)))

    def forward(s):
        for i in (2, 1, 3):
            block = tok.at[s, shift(-i, 0)]
            wait_for(block, ag1a_recv.at[s, i - 1])
            for j in (2, 1, 3):
                remote(block, block, ag1_send.at[s], ag1b_recv.at[s], (r, shift(0, j)))

    def m1(s):
        if s == 0:
            loads[0].wait()
        wait_for(tok.at[s, pl.ds(0, 15 if DIRECT[s] else 12)], ag1b_recv.at[s])
        left = tok[s].reshape(NC * ROWS, width)
        part = jnp.dot(left, w[...], preferred_element_type=F32).astype(BF16)
        pp[s] = part.reshape(NZ, 2, ROWS, hidden)
        for q in NEED:
            d = at_z(q)
            remote(pp.at[s, d, other], px.at[s, d], px_send.at[s], px_recv.at[s, abs(q)], partner)

    def base(s, d):
        return pp[s, d, k].astype(F32) + px[s, d].astype(F32)

    def r4(s):
        wait_for(px.at[s, 0], px_recv.at[s, 4])
        s4[s] = base(s, at_z(4)).astype(BF16)
        remote(s4.at[s, :, lo], rp.at[s, 3, :, lo], rs_send.at[s, 0], rp_recv.at[s, 3], up)
        remote(s4.at[s, :, hi], rm.at[s, 3, :, hi], rs_send.at[s, 1], rm_recv.at[s, 3], down)

    def r3(s):
        wait_for(px.at[s, pl.ds(0, 2)], px_recv.at[s, 3])
        wait_for(rp.at[s, 3, :, lo], rp_recv.at[s, 3])
        up_sum = base(s, at_z(3))
        sp[s, 3, :, lo] = (up_sum[:, :half] + rp[s, 3, :, lo].astype(F32)).astype(BF16)
        sp[s, 3, :, hi] = up_sum[:, half:].astype(BF16)
        remote(sp.at[s, 3], rp.at[s, 2], rs_send.at[s, 2], rp_recv.at[s, 2], up)
        wait_for(rm.at[s, 3, :, hi], rm_recv.at[s, 3])
        down_sum = base(s, at_z(-3))
        sm[s, 3, :, hi] = (down_sum[:, half:] + rm[s, 3, :, hi].astype(F32)).astype(BF16)
        sm[s, 3, :, lo] = down_sum[:, :half].astype(BF16)
        remote(sm.at[s, 3], rm.at[s, 2], rs_send.at[s, 3], rm_recv.at[s, 2], down)

    def rj(s, j):
        wait_for(px.at[s, pl.ds(0, 2)], px_recv.at[s, j])
        up_sum, down_sum = base(s, at_z(j)), base(s, at_z(-j))
        wait_for(rp.at[s, j], rp_recv.at[s, j])
        sp[s, j] = (up_sum + rp[s, j].astype(F32)).astype(BF16)
        remote(sp.at[s, j], rp.at[s, j - 1], rs_send.at[s, 8 - 2 * j], rp_recv.at[s, j - 1], up)
        wait_for(rm.at[s, j], rm_recv.at[s, j])
        sm[s, j] = (down_sum + rm[s, j].astype(F32)).astype(BF16)
        remote(sm.at[s, j], rm.at[s, j - 1], rs_send.at[s, 9 - 2 * j], rm_recv.at[s, j - 1], down)

    def r0(s):
        wait_for(px.at[s, 0], px_recv.at[s, 0])
        wait_for(rp.at[s, 0], rp_recv.at[s, 0])
        wait_for(rm.at[s, 0], rm_recv.at[s, 0])
        if s == 0:
            loads[1].wait()
        rows = pl.ds(s * ROWS, ROWS)
        pre = base(s, z) + rp[s, 0].astype(F32) + rm[s, 0].astype(F32)
        activated, slope = gelu_pair(pre)
        g[s, z, k] = (cot[rows].astype(F32) * slope).astype(BF16)
        mine = g.at[s, z, k]
        remote(mine, mine, ag_send.at[s, 0], gp_recv.at[s, 0], up)
        remote(mine, mine, ag_send.at[s, 1], gm_recv.at[s, 0], down)
        remote(mine, mine, pt_send.at[s], pt_recv.at[s, 0], partner)
        act[rows] = activated.astype(BF16)

    def a(s, j):
        below, above = g.at[s, at_z(-j), k], g.at[s, at_z(j), k]
        if j < 3:
            wait_for(below, gp_recv.at[s, j - 1])
            remote(below, below, ag_send.at[s, 2 * j], gp_recv.at[s, j], up)
            wait_for(above, gm_recv.at[s, j - 1])
            remote(above, above, ag_send.at[s, 2 * j + 1], gm_recv.at[s, j], down)
        else:
            wait_for(below, gp_recv.at[s, j - 1])
            part = g.at[s, at_z(-j), k, :, lo]
            remote(part, part, ag_send.at[s, 2 * j], gp_recv.at[s, j], up)
            wait_for(above, gm_recv.at[s, j - 1])
            part = g.at[s, at_z(j), k, :, hi]
            remote(part, part, ag_send.at[s, 2 * j + 1], gm_recv.at[s, j], down)
        remote(below, below, pt_send.at[s], pt_recv.at[s, 2 * j - 1], partner)
        remote(above, above, pt_send.at[s], pt_recv.at[s, 2 * j], partner)

    def a4(s):
        far = g.at[s, at_z(4), k]
        wait_for(g.at[s, at_z(4), k, :, lo], gp_recv.at[s, 3])
        wait_for(g.at[s, at_z(4), k, :, hi], gm_recv.at[s, 3])
        remote(far, far, pt_send.at[s], pt_recv.at[s, 7], partner)

    def pass_on(s):
        wait_for(r2.at[s, pl.ds(0, 12)], r2_recv.at[s])
        for j in (2, 1, 3, 0):
            total = ip[s, shift(0, j)].astype(F32)
            for i in range(3):
                total += r2[s, 4 * i + j].astype(F32)
            if j == 0:
                t0[s] = total
            else:
                t1[s, j - 1] = total.astype(BF16)
                remote(t1.at[s, j - 1], r2.at[s, 11 + j], r2b_send.at[s], r2b_recv.at[s], (r, shift(0, j)))

    def m2_part(s, chunks):
        for q, slot in chunks:
            wait_for(g.at[s, 0, 0], pt_recv.at[s, slot])
        if len(chunks) == NZ:
            left = g[s].reshape(NR * ROWS, hidden)
        else:
            left = jnp.concatenate(
                [g[s, at_z(q)].reshape(2 * ROWS, hidden) for q, _ in chunks], axis=0
            )
        part = lax.dot_general(
            left, w[...], (((1,), (1,)), ((), ())), preferred_element_type=F32
        ).astype(BF16)
        part = part.reshape(len(chunks), 2, ROWS, width)
        if len(chunks) == NZ:
            ip[s] = part.reshape(NC, ROWS, width)
        for n, (q, _) in enumerate(chunks):
            d = at_z(q)
            if len(chunks) < NZ:
                ip[s, pl.ds(2 * d, 2)] = part[n]
            for m in range(2):
                dest = 2 * d + m
                if TWO[s]:
                    i, j = offsets(dest)

                    @pl.when(i != 0)
                    def _():
                        slot = 4 * i - 4 + j
                        remote(ip.at[s, dest], r2.at[s, slot], r2_send.at[s], r2_recv.at[s], (r, shift(i, 0)))
                else:

                    @pl.when(dest != c)
                    def _():
                        slot = lax.rem(dest - c + NC, NC) - 1
                        remote(ip.at[s, dest], r2.at[s, slot], r2_send.at[s], r2_recv.at[s], (r, dest))

    def leave_sum(s):
        rows = pl.ds(s * ROWS, ROWS)
        pltpu.make_async_copy(ig.at[rows], ig_ref.at[rows], out_sem.at[2]).start()

    def fin(s):
        if TWO[s]:
            wait_for(r2.at[s, pl.ds(12, 3)], r2b_recv.at[s])
            total = t0[s]
            for j in range(3):
                total += r2[s, 12 + j].astype(F32)
            ig[pl.ds(s * ROWS, ROWS)] = total.astype(BF16)
            return leave_sum(s)
        wait_for(r2.at[s], r2_recv.at[s])
        total = ip[s, c].astype(F32)
        for i in range(NC - 1):
            total += r2[s, i].astype(F32)
        ig[pl.ds(s * ROWS, ROWS)] = total.astype(BF16)
        leave_sum(s)

    def wgrad(part):
        some = pl.ds(2 * part, 2)

        def body(j, carry):
            cols = pl.ds(pl.multiple_of(j * TILE, TILE), TILE)
            left = tok[some].reshape(2 * NC * ROWS, width)
            right = g[some, :, :, :, cols].reshape(2 * NR * ROWS, TILE)
            total = lax.dot_general(
                left, right, (((0,), (0,)), ((), ())), preferred_element_type=F32
            )
            if part == 0:
                acc[:, cols] = total
            else:
                wg[:, cols] = (acc[:, cols] + total).astype(BF16)
                pltpu.make_async_copy(wg.at[:, cols], wg_ref.at[:, cols], out_sem.at[1]).start()
            return carry

        lax.fori_loop(0, hidden // TILE, body, 0)

    def product(s, n):
        chunks = []
        for j in CUTS[PIECES[s]][n]:
            chunks += [(0, 0)] if j == 0 else [(4, 7)] if j == 4 else [(-j, 2 * j - 1), (j, 2 * j)]
        m2_part(s, chunks)

    outs = [
        pltpu.make_async_copy(a_v, b_v, out_sem.at[n])
        for n, (a_v, b_v) in enumerate(((act, act_ref), (wg, wg_ref), (ig, ig_ref)))
    ]

    def start_wgrad(part):
        if part == 0:
            outs[0].start()
        wgrad(part)

    def settle(_):
        for s in range(stages):
            wait_for(tok.at[s, pl.ds(0, NC - 1)], ag1_send.at[s])
            wait_for(px.at[s], px_send.at[s])
            wait_for(s4.at[s, :, lo], rs_send.at[s, 0])
            wait_for(s4.at[s, :, hi], rs_send.at[s, 1])
            for j in range(2, 8):
                wait_for(s4.at[s], rs_send.at[s, j])
            for j in range(6):
                wait_for(s4.at[s], ag_send.at[s, j])
            wait_for(s4.at[s, :, lo], ag_send.at[s, 6])
            wait_for(s4.at[s, :, hi], ag_send.at[s, 7])
            wait_for(g.at[s, :, 0], pt_send.at[s])
            if TWO[s]:
                wait_for(r2.at[s, pl.ds(0, 12)], r2_send.at[s])

    step = {"O": own, "F": forward, "M": m1, "R4": r4, "R3": r3, "R0": r0, "A4": a4, "P": pass_on, "FIN": fin, "WG": start_wgrad, "W": settle}
    for j in (1, 2):
        step[f"R{j}"] = functools.partial(lambda j, s: rj(s, j), j)
    for j in (1, 2, 3):
        step[f"A{j}"] = functools.partial(lambda j, s: a(s, j), j)
    for n in range(4):
        step[f"N{n}"] = functools.partial(lambda n, s: product(s, n), n)
    for name, s in ORDER:
        step[name](s)

    for s in range(stages):
        if TWO[s]:
            wait_for(r2.at[s, pl.ds(12, 3)], r2b_send.at[s])
        else:
            wait_for(r2.at[s], r2_send.at[s])
    for cp in outs:
        cp.wait()


def copy_kernel(*refs):
    copies = [pltpu.make_async_copy(refs[n], refs[3 + n], refs[6].at[n]) for n in range(3)]
    for cp in copies:
        cp.start()
    for cp in copies:
        cp.wait()


def kern(tokens, weight, cotangent):
    rows, width = tokens.shape
    hidden = weight.shape[1]
    stages = rows // ROWS
    vmem, dma = pltpu.VMEM, pltpu.SemaphoreType.DMA
    any_spec = pl.BlockSpec(memory_space=pl.ANY)
    return pl.pallas_call(
        functools.partial(kernel, stages),
        out_shape=(
            jax.ShapeDtypeStruct((rows, hidden), BF16),
            jax.ShapeDtypeStruct((rows, width), BF16),
            jax.ShapeDtypeStruct((width, hidden), BF16),
        ),
        in_specs=[any_spec] * 3,
        out_specs=(any_spec,) * 3,
        scratch_shapes=[
            vmem((width, hidden), BF16),
            vmem((rows, hidden), BF16),
            vmem((stages, NC, ROWS, width), BF16),
            vmem((stages, NZ, 2, ROWS, hidden), BF16),
            vmem((stages, NZ, ROWS, hidden), BF16),
            vmem((stages, ROWS, hidden), BF16),
            vmem((stages, 4, ROWS, hidden), BF16),
            vmem((stages, 4, ROWS, hidden), BF16),
            vmem((stages, 4, ROWS, hidden), BF16),
            vmem((stages, 4, ROWS, hidden), BF16),
            vmem((stages, NZ, 2, ROWS, hidden), BF16),
            vmem((stages, NC, ROWS, width), BF16),
            vmem((stages, NC - 1, ROWS, width), BF16),
            vmem((stages, ROWS, width), F32),
            vmem((stages, 3, ROWS, width), BF16),
            vmem((rows, hidden), BF16),
            vmem((rows, width), BF16),
            vmem((width, hidden), BF16),
            vmem((width, hidden), F32),
            dma((2 + stages,)), dma((3,)),
            dma((stages,)), dma((stages, 3)), dma((stages,)), dma((stages,)), dma((stages, 5)),
            dma((stages, 8)), dma((stages, 4)), dma((stages, 4)),
            dma((stages, 8)), dma((stages, 4)), dma((stages, 4)),
            dma((stages,)), dma((stages, 8)),
            dma((stages,)), dma((stages,)), dma((stages,)), dma((stages,)),
        ],
        compiler_params=pltpu.CompilerParams(
            collective_id=0, has_side_effects=True, vmem_limit_bytes=50 * 2**20
        ),
        name="updown",
    )(tokens, weight, cotangent)


def on_device(tokens, weight, cotangent):
    tokens, weight, cotangent = (
        pltpu.with_memory_space_constraint(v, pltpu.HBM) for v in (tokens, weight, cotangent)
    )
    outs = kern(tokens, weight, cotangent)
    any_spec, dma = pl.BlockSpec(memory_space=pl.ANY), pltpu.SemaphoreType.DMA
    return tuple(pl.pallas_call(
        copy_kernel,
        out_shape=tuple(jax.ShapeDtypeStruct(o.shape, o.dtype) for o in outs),
        in_specs=[any_spec] * 3,
        out_specs=(any_spec,) * 3,
        scratch_shapes=[dma((3,))],
        compiler_params=pltpu.CompilerParams(vmem_limit_bytes=16 * 2**20),
        name="leave",
    )(*outs))


def solution(mesh):
    return jax.shard_map(
        on_device,
        mesh=mesh,
        in_specs=(P("col", "row"), P("row", "col"), P("row", "col")),
        out_specs=(P("row", "col"), P("col", "row"), P("row", "col")),
        check_vma=False,
    )
```
